32 devices in a mesh: grp: 4 (over x, core), rep: 8 (over z, y).
Axes of the slice: x: 2, y: 2, z: 4, core: 2. Of those that a mesh axis runs over, the one named last changes fastest.
Arguments:
- hidden_in: bfloat16 [8, 1024, 1024], P('rep', 'grp'), may hold values from -6 to 6
- doc_ids: int32 [8, 1024], P('rep'), may hold values from 0 to 3, never falling along the last dimension, each value on 1 to 512 neighbouring positions
- ln1_gain: bfloat16 [1024], P('grp'), may hold values from 0.099609375 to 1.8984375
- ln1_bias: bfloat16 [1024], P('grp'), may hold values from -4 to 4
- ln2_gain: bfloat16 [1024], P('grp'), may hold values from 0.099609375 to 1.8984375
- ln2_bias: bfloat16 [1024], P('grp'), may hold values from -4 to 4
- qkv_weight: bfloat16 [1024, 3072], P('grp'), may hold values from -0.1875 to 0.1875
- qkv_bias: bfloat16 [3072], P('grp'), may hold values from -4 to 4
- dense_weight: bfloat16 [1024, 1024], P('grp'), may hold values from -1.5 to 1.5
- dense_bias: bfloat16 [1024], P('grp'), may hold values from -4 to 4
- fc1_weight: bfloat16 [1024, 4096], P('grp'), may hold values from -0.1875 to 0.1875
- fc1_bias: bfloat16 [4096], P('grp'), may hold values from -4 to 4
- fc2_weight: bfloat16 [4096, 1024], P('grp'), may hold values from -0.09375 to 0.09375
- fc2_bias: bfloat16 [1024], P('grp'), may hold values from -4 to 4
- out_grad: bfloat16 [8, 1024, 1024], P('rep', 'grp'), may hold values from -6 to 6
Outputs:
- hidden_out: bfloat16 [8, 1024, 1024], P('rep', 'grp')
- hidden_grad: bfloat16 [8, 1024, 1024], P('rep', 'grp')
- ln1_gain_grad: float32 [1024], P('grp')
- ln1_bias_grad: float32 [1024], P('grp')
- ln2_gain_grad: float32 [1024], P('grp')
- ln2_bias_grad: float32 [1024], P('grp')
- qkv_weight_grad: float32 [1024, 3072], P('grp')
- qkv_bias_grad: float32 [3072], P('grp')
- dense_weight_grad: float32 [1024, 1024], P('grp')
- dense_bias_grad: float32 [1024], P('grp')
- fc1_weight_grad: float32 [1024, 4096], P('grp')
- fc1_bias_grad: float32 [4096], P('grp')
- fc2_weight_grad: float32 [4096, 1024], P('grp')
- fc2_bias_grad: float32 [1024], P('grp')
The draws below stay inside these ranges and needn't reach their ends.
Inputs may be any that keep to these rules, and one draw needn't show every extreme that they name: `doc_ids`: document numbers never fall along a sequence; each of the 4 documents of a sequence has 1 to 512 tokens, and one has exactly that many.
All inputs are finite; a program needn't handle non-finite values.
Results may differ from the reference program's by a relative error of at most 0.025.
Values may be sent and summed in bfloat16 or wider, within the bound.
A program may use at most 192 MiB of HBM per device.

```python
import math
import jax
import jax.numpy as jnp
import numpy as np
from jax import lax

D = 1024
HEADS = 16
HEAD_DIM = 64
FF = 4096
ROT = 16
DOCS = 4
LENGTH = 1024
SEQS = 8


def block_scale(stream_key, shape, cuts, least, largest):
    def one(axis_at, shards_of):
        steps = jax.random.uniform(jax.random.fold_in(jax.random.fold_in(stream_key, 6), axis_at), (shards_of,), jnp.float32, least / len(cuts), largest / len(cuts))
        return jnp.repeat(jnp.exp(steps), shape[axis_at] // shards_of).reshape((-1,) + (1,) * (len(shape) - axis_at - 1))

    level = one(*cuts[0])
    for cut in cuts[1:]:
        level = level * one(*cut)
    return level


def length_profile(number_of, total, bound, lean):
    weights = [(1 << 20) // math.isqrt(grade ** lean) + 1 for grade in range(2, number_of + 1)]
    spare, given = total - bound - (number_of - 1), [1] * (number_of - 1)
    while spare > 0:
        candidates = [i for i in range(number_of - 1) if given[i] < bound]
        whole, budget = sum([weights[i] for i in candidates]), spare
        for i in candidates:
            extra = min(bound - given[i], max(1, budget * weights[i] // whole), spare)
            given[i] = given[i] + extra
            spare = spare - extra
    return np.array([bound] + given)


def ragged(own_key, count, total, bound, skew):
    if count == 2:
        one = jax.random.randint(own_key, (), max(1, total - bound), min(bound, total - 1) + 1)
        return jnp.stack([one, total - one])
    sizes = jnp.asarray(length_profile(count, total, bound, skew), jnp.int32)
    couples = (count - 1) // 2
    donor, taker = sizes[1:1 + 2 * couples:2], sizes[2:2 + 2 * couples:2]
    margin = jnp.minimum(donor - 1, bound - taker)
    shifted = jax.random.randint(jax.random.fold_in(own_key, 1), (couples,), 0, 1 << 20) % (margin + 1)
    sizes = sizes.at[1:1 + 2 * couples:2].set(donor - shifted).at[2:2 + 2 * couples:2].set(taker + shifted)
    return sizes[jax.random.permutation(jax.random.fold_in(own_key, 2), count)]


def noise(key, dims, scale, bound, cuts=(), held_as=jnp.bfloat16):
    array = scale * jax.random.normal(key, dims, jnp.float32)
    if cuts:
        array = array * block_scale(key, dims, cuts, -0.22, 0.18)
    return jnp.clip(array, -bound, bound).astype(held_as)


def setup_inputs(seed: int = 0) -> dict:
    arg_keys = jax.random.split(jax.random.key(seed), 16)
    hidden_in = noise(arg_keys[0], (SEQS, LENGTH, D), 1.0, 6.0, ((0, 8), (1, 4)))
    doc_ids = jax.vmap(lambda own: jnp.searchsorted(jnp.cumsum(ragged(own, DOCS, LENGTH, LENGTH // 2, 0)), jnp.arange(LENGTH), side="right"))(jax.random.split(arg_keys[1], SEQS)).reshape((SEQS, LENGTH)).astype(jnp.int32)
    ln1_gain = jnp.clip(1.0 + 0.18 * jax.random.normal(arg_keys[2], (D,), jnp.float32), 0.099609375, 1.8984375).astype(jnp.bfloat16)
    ln1_bias = noise(arg_keys[3], (D,), 1.0, 4.0, ((0, 4),))
    ln2_gain = jnp.clip(1.0 + 0.18 * jax.random.normal(arg_keys[4], (D,), jnp.float32), 0.099609375, 1.8984375).astype(jnp.bfloat16)
    ln2_bias = noise(arg_keys[5], (D,), 1.0, 4.0, ((0, 4),))
    qkv_weight = noise(arg_keys[6], (D, 3 * D), D ** -0.5, 0.1875, ((0, 4),))
    qkv_bias = noise(arg_keys[7], (3 * D,), 1.0, 4.0, ((0, 4),))
    dense_weight = noise(arg_keys[8], (D, D), (D // 64) ** -0.5, 1.5, ((0, 4),))
    dense_bias = noise(arg_keys[9], (D,), 1.0, 4.0, ((0, 4),))
    fc1_weight = noise(arg_keys[10], (D, FF), D ** -0.5, 0.1875, ((0, 4),))
    fc1_bias = noise(arg_keys[11], (FF,), 1.0, 4.0, ((0, 4),))
    fc2_weight = noise(arg_keys[12], (FF, D), FF ** -0.5, 0.09375, ((0, 4),))
    fc2_bias = noise(arg_keys[13], (D,), 1.0, 4.0, ((0, 4),))
    out_grad = noise(arg_keys[14], (SEQS, LENGTH, D), 1.0, 6.0, ((0, 8), (1, 4)))
    return dict(hidden_in=hidden_in, doc_ids=doc_ids, ln1_gain=ln1_gain, ln1_bias=ln1_bias, ln2_gain=ln2_gain, ln2_bias=ln2_bias, qkv_weight=qkv_weight, qkv_bias=qkv_bias, dense_weight=dense_weight, dense_bias=dense_bias, fc1_weight=fc1_weight, fc1_bias=fc1_bias, fc2_weight=fc2_weight, fc2_bias=fc2_bias, out_grad=out_grad)


EPS = 1e-05
NEG = -1e+30

def layer_norm_forward(x, norm_gain_vector, norm_offset_bias):
    row_average = lax.optimization_barrier(jnp.mean(x, axis=-1, keepdims=True))
    centered_input = x - row_average
    var = lax.optimization_barrier(jnp.mean(centered_input * centered_input, axis=-1, keepdims=True))
    inverse_deviation = lax.rsqrt(var + EPS)
    normalized_input = centered_input * inverse_deviation
    return (normalized_input * norm_gain_vector.astype(jnp.float32) + norm_offset_bias.astype(jnp.float32), normalized_input, inverse_deviation)

def layer_norm_backward(output_gradient, normalized_input, inverse_deviation, norm_gain_vector):
    gain_scaled_grad = output_gradient * norm_gain_vector.astype(jnp.float32)
    projection_term = gain_scaled_grad - lax.optimization_barrier(jnp.mean(gain_scaled_grad, axis=-1, keepdims=True)) - normalized_input * lax.optimization_barrier(jnp.mean(gain_scaled_grad * normalized_input, axis=-1, keepdims=True))
    return (inverse_deviation * projection_term, lax.optimization_barrier(jnp.sum(output_gradient * normalized_input, axis=0)), lax.optimization_barrier(jnp.sum(output_gradient, axis=0)))

def rotary_tables(positions, rot):
    half = rot // 2
    freq = 10000.0 ** (-jnp.arange(half, dtype=jnp.float32) / half)
    angle = positions.astype(jnp.float32)[:, None] * freq[None, :]
    return (jnp.cos(angle), jnp.sin(angle))

def rotate(x, cosine, sine, sign):
    half = cosine.shape[1]
    first = x[..., :half]
    second = x[..., half:2 * half]
    cwide = cosine[:, None, :]
    swide = sign * sine[:, None, :]
    return jnp.concatenate([first * cwide - second * swide, second * cwide + first * swide, x[..., 2 * half:]], axis=-1)

def gelu_parts(pre):
    cdf = 0.5 * (1.0 + jax.scipy.special.erf(pre * (1.0 / math.sqrt(2.0))))
    dens = jnp.exp(-0.5 * pre * pre) * (1.0 / math.sqrt(2.0 * math.pi))
    return (pre * cdf, cdf + pre * dens)

def one_sequence(x, docs, dy, params):
    first_norm_gain, first_norm_bias, second_norm_gain, second_norm_bias, wqkv, bqkv, wd, bd, w1, bf1, w2, bf2 = params
    length, width = x.shape
    heads = HEADS
    hdim = HEAD_DIM
    scale = hdim ** (-0.5)
    f32 = jnp.float32
    bf16 = jnp.bfloat16
    input_single_precision = x.astype(f32)
    first_hidden_state, first_normalized_input, first_inverse_deviation = layer_norm_forward(input_single_precision, first_norm_gain, first_norm_bias)
    second_hidden_state, second_normalized_input, second_inverse_deviation = layer_norm_forward(input_single_precision, second_norm_gain, second_norm_bias)
    a1 = first_hidden_state.astype(bf16)
    a2 = second_hidden_state.astype(bf16)
    qkv = jnp.dot(a1, wqkv, preferred_element_type=f32) + bqkv.astype(f32)
    pos = jnp.arange(length, dtype=jnp.int32)
    cosine, sine = rotary_tables(pos, ROT)
    query = rotate(qkv[:, :width].reshape(length, heads, hdim), cosine, sine, 1.0).astype(bf16)
    keyrot = rotate(qkv[:, width:2 * width].reshape(length, heads, hdim), cosine, sine, 1.0).astype(bf16)
    value = qkv[:, 2 * width:].reshape(length, heads, hdim).astype(bf16)
    mask = (pos[None, :] <= pos[:, None]) & (docs[None, :] == docs[:, None])
    scores = jnp.einsum('qhd,khd->hqk', query.astype(f32), keyrot.astype(f32)) * scale
    scores = jnp.where(mask[None], scores, NEG)
    top = lax.optimization_barrier(jnp.max(scores, axis=-1, keepdims=True))
    lse = top + jnp.log(lax.optimization_barrier(jnp.sum(jnp.exp(scores - top), axis=-1, keepdims=True)))
    prob = jnp.exp(scores - lse)
    prob_b = prob.astype(bf16)
    mixed = jnp.einsum('hqk,khd->qhd', prob_b.astype(f32), value.astype(f32)).astype(bf16)
    mixed_flat = mixed.reshape(length, width)
    attn = jnp.dot(mixed_flat, wd, preferred_element_type=f32) + bd.astype(f32)
    pre = jnp.dot(a2, w1, preferred_element_type=f32) + bf1.astype(f32)
    act, slope = gelu_parts(pre)
    gact = act.astype(bf16)
    mlp = jnp.dot(gact, w2, preferred_element_type=f32) + bf2.astype(f32)
    out = (input_single_precision + attn + mlp).astype(bf16)
    dyf = dy.astype(f32)
    dw2 = jnp.dot(gact.T, dy, preferred_element_type=f32)
    dbias_out = lax.optimization_barrier(jnp.sum(dyf, axis=0))
    dpre = jnp.dot(dy, w2.T, preferred_element_type=f32) * slope
    dbf1 = lax.optimization_barrier(jnp.sum(dpre, axis=0))
    dpre_b = dpre.astype(bf16)
    dw1 = jnp.dot(a2.T, dpre_b, preferred_element_type=f32)
    second_mlp_input_grad = jnp.dot(dpre_b, w1.T, preferred_element_type=f32)
    dwd = jnp.dot(mixed_flat.T, dy, preferred_element_type=f32)
    dmix = jnp.dot(dy, wd.T, preferred_element_type=f32).astype(bf16).reshape(length, heads, hdim)
    delta = lax.optimization_barrier(jnp.sum(dmix.astype(f32) * mixed.astype(f32), axis=-1))
    dprob = jnp.einsum('qhd,khd->hqk', dmix.astype(f32), value.astype(f32))
    dscore = (prob * (dprob - delta.T[:, :, None]) * scale).astype(bf16)
    dquery = jnp.einsum('hqk,khd->qhd', dscore.astype(f32), keyrot.astype(f32))
    dkey = jnp.einsum('hqk,qhd->khd', dscore.astype(f32), query.astype(f32))
    dvalue = jnp.einsum('hqk,qhd->khd', prob_b.astype(f32), dmix.astype(f32))
    dquery = rotate(dquery, cosine, sine, -1.0)
    dkey = rotate(dkey, cosine, sine, -1.0)
    dqkv = jnp.concatenate([dquery.reshape(length, width), dkey.reshape(length, width), dvalue.reshape(length, width)], axis=1)
    dbqkv = lax.optimization_barrier(jnp.sum(dqkv, axis=0))
    dqkv_b = dqkv.astype(bf16)
    dwqkv = jnp.dot(a1.T, dqkv_b, preferred_element_type=f32)
    first_attn_input_grad = jnp.dot(dqkv_b, wqkv.T, preferred_element_type=f32)
    first_residual_grad, first_norm_gain_grad, first_norm_bias_grad = layer_norm_backward(first_attn_input_grad, first_normalized_input, first_inverse_deviation, first_norm_gain)
    second_residual_grad, second_norm_gain_grad, second_norm_bias_grad = layer_norm_backward(second_mlp_input_grad, second_normalized_input, second_inverse_deviation, second_norm_gain)
    dx = (dyf + first_residual_grad + second_residual_grad).astype(bf16)
    grads = (first_norm_gain_grad, first_norm_bias_grad, second_norm_gain_grad, second_norm_bias_grad, dwqkv, dbqkv, dwd, dbias_out, dw1, dbf1, dw2, dbias_out)
    return (out, dx, grads)

def reference(hidden_in, doc_ids, ln1_gain, ln1_bias, ln2_gain, ln2_bias, qkv_weight, qkv_bias, dense_weight, dense_bias, fc1_weight, fc1_bias, fc2_weight, fc2_bias, out_grad):
    params = (ln1_gain, ln1_bias, ln2_gain, ln2_bias, qkv_weight, qkv_bias, dense_weight, dense_bias, fc1_weight, fc1_bias, fc2_weight, fc2_bias)

    def step(carry, item):
        x, docs, dy = item
        out, dx, grads = one_sequence(x, docs, dy, params)
        return (tuple((c + g for c, g in zip(carry, grads))), (out, dx))
    init = tuple((jnp.zeros(p.shape, jnp.float32) for p in params))
    sums, pair = lax.scan(step, init, (hidden_in, doc_ids, out_grad))
    outs, dxs = pair
    return (outs, dxs, sums[0], sums[1], sums[2], sums[3], sums[4], sums[5], sums[6], sums[7], sums[8], sums[9], sums[10], sums[11])
```

```python
import functools
import math

import jax
import jax.numpy as jnp
import numpy as np
from jax import lax
from jax.experimental import pallas as pl
from jax.experimental.pallas import tpu as pltpu
from jax.sharding import PartitionSpec as P

HEAD_DIM = 64
ROT = 16
EPS = 1e-05
NEG = -1e30
DOC_MAX = 512
PAIR = 128

f32 = jnp.float32
bf16 = jnp.bfloat16


def rotary_tables(length):
    half = ROT // 2
    freq = 10000.0 ** (-np.arange(half, dtype=np.float64) / half)
    angle = np.arange(length, dtype=np.float64)[:, None] * freq[None, :]
    cos = np.ones((length, HEAD_DIM))
    low = np.zeros((length, HEAD_DIM))
    high = np.zeros((length, HEAD_DIM))
    cos[:, :half] = np.cos(angle)
    cos[:, half : 2 * half] = np.cos(angle)
    low[:, :half] = -np.sin(angle)
    high[:, half : 2 * half] = np.sin(angle)
    reps = PAIR // HEAD_DIM
    return tuple(np.tile(t, (1, reps)).astype(np.float32) for t in (cos, low, high))


def rotate(x, cos, low, high, sign):
    half = ROT // 2
    up = pltpu.roll(x, PAIR - half, 1)
    down = pltpu.roll(x, half, 1)
    return x * cos + sign * (up * low + down * high)


def dot_nt(a, b):
    return lax.dot_general(a, b, (((1,), (1,)), ((), ())), preferred_element_type=f32)


def dot_tn(a, b):
    return lax.dot_general(a, b, (((0,), (0,)), ((), ())), preferred_element_type=f32)


def attention_kernel(
    block,
    q_ref,
    k_ref,
    v_ref,
    dmix_ref,
    drow_ref,
    dcol_ref,
    cos_ref,
    low_ref,
    high_ref,
    mix_ref,
    dq_ref,
    dk_ref,
    dv_ref,
    bias_ref,
    qs,
    ks,
    vs,
    dks,
    dvs,
):
    length = q_ref.shape[0]
    scale = HEAD_DIM ** (-0.5)
    tables = (cos_ref[...], low_ref[...], high_ref[...])
    qs[...] = rotate(q_ref[...], *tables, 1.0).astype(bf16)
    ks[...] = rotate(k_ref[...], *tables, 1.0).astype(bf16)
    vs[...] = v_ref[...].astype(bf16)
    dks[...] = jnp.zeros_like(dks)
    dvs[...] = jnp.zeros_like(dvs)
    dq_sum = jnp.zeros((1, PAIR), f32)
    reach = -(-(DOC_MAX - 1) // block)
    for i in range(length // block):
        first = max(0, i - reach) * block
        end = (i + 1) * block
        wide = end - first
        rows = pl.ds(i * block, block)
        keys = pl.ds(first, wide)
        q = qs[rows, :]
        dmix = dmix_ref[rows, :]
        k = ks[keys, :]
        v = vs[keys, :]
        qpos = i * block + lax.broadcasted_iota(jnp.int32, (block, wide), 0)
        kpos = first + lax.broadcasted_iota(jnp.int32, (block, wide), 1)
        allowed = (kpos <= qpos) & (dcol_ref[rows, :] == drow_ref[:, first:end])
        lane = lax.broadcasted_iota(jnp.int32, (block, PAIR), 1)
        wide_lane = lax.broadcasted_iota(jnp.int32, (wide, PAIR), 1)
        mix = dq = None
        for h in range(PAIR // HEAD_DIM):
            mine = (lane // HEAD_DIM) == h
            zero = jnp.zeros((block, PAIR), bf16)
            qh = jnp.where(mine, q, zero)
            dmixh = jnp.where(mine, dmix, zero)
            s = jnp.where(allowed, dot_nt(qh, k) * scale, NEG)
            top = jnp.max(s, axis=1, keepdims=True)
            e = jnp.exp(s - top)
            p = e * (1.0 / jnp.sum(e, axis=1, keepdims=True))
            pb = p.astype(bf16)
            o = jnp.dot(pb, v, preferred_element_type=f32).astype(bf16)
            o = jnp.where(mine, o, zero)
            delta = jnp.sum(o.astype(f32) * dmixh.astype(f32), axis=1, keepdims=True)
            dp = dot_nt(dmixh, v)
            ds = (p * (dp - delta) * scale).astype(bf16)
            dqh = jnp.dot(ds, k, preferred_element_type=f32)
            mix = o if h == 0 else mix + o
            dq = jnp.where(mine, dqh, 0.0) if h == 0 else jnp.where(mine, dqh, dq)
            dks[keys, :] += dot_tn(ds, qh)
            dvs[keys, :] += dot_tn(pb, dmixh)
        mix_ref[rows, :] = mix
        dq = rotate(dq, cos_ref[rows, :], low_ref[rows, :], high_ref[rows, :], -1.0)
        dq_sum = dq_sum + jnp.sum(dq, axis=0, keepdims=True)
        dq_ref[rows, :] = dq.astype(bf16)
    dk = rotate(dks[...], *tables, -1.0)
    dv = dvs[...]
    dk_ref[...] = dk.astype(bf16)
    dv_ref[...] = dv.astype(bf16)
    bias_ref[0:1, :] = dq_sum
    bias_ref[1:2, :] = jnp.sum(dk, axis=0, keepdims=True)
    bias_ref[2:3, :] = jnp.sum(dv, axis=0, keepdims=True)
    bias_ref[3:8, :] = jnp.zeros((5, PAIR), f32)


def attention(qkv, dmix, docs):
    length, width = dmix.shape
    pairs = width // PAIR
    block = 256
    col = lambda off: pl.BlockSpec((length, PAIR), lambda h: (0, off + h))
    whole = lambda shape: pl.BlockSpec(shape, lambda h: (0, 0))
    tables = [jnp.asarray(t) for t in rotary_tables(length)]
    out = lambda: jax.ShapeDtypeStruct((length, width), bf16)
    return pl.pallas_call(
        functools.partial(attention_kernel, block),
        grid=(pairs,),
        in_specs=[col(0), col(pairs), col(2 * pairs), col(0)]
        + [whole((1, length)), whole((length, 1))]
        + [whole((length, PAIR))] * 3,
        out_specs=[col(0)] * 4 + [pl.BlockSpec((8, PAIR), lambda h: (0, h))],
        out_shape=[out(), out(), out(), out(), jax.ShapeDtypeStruct((8, width), f32)],
        scratch_shapes=[pltpu.VMEM((length, PAIR), bf16)] * 3
        + [pltpu.VMEM((length, PAIR), f32)] * 2,
        compiler_params=pltpu.CompilerParams(vmem_limit_bytes=40 * 1024 * 1024),
        cost_estimate=pl.CostEstimate(
            flops=10 * length * length * width, bytes_accessed=length * width * 24, transcendentals=length * length * 4
        ),
    )(qkv, qkv, qkv, dmix, docs[None, :], docs[:, None], *tables)


def gelu_parts(pre):
    cdf = 0.5 * (1.0 + lax.erf(pre * (1.0 / math.sqrt(2.0))))
    dens = jnp.exp(-0.5 * pre * pre) * (1.0 / math.sqrt(2.0 * math.pi))
    return (pre * cdf, cdf + pre * dens)


def body(
    groups,
    reps,
    hidden_in,
    doc_ids,
    ln1_gain,
    ln1_bias,
    ln2_gain,
    ln2_bias,
    qkv_weight,
    qkv_bias,
    dense_weight,
    dense_bias,
    fc1_weight,
    fc1_bias,
    fc2_weight,
    fc2_bias,
    out_grad,
):
    own = lax.axis_index("grp")
    x_own = hidden_in[0]
    dy_own = out_grad[0]
    docs = doc_ids[0]
    rows, width = x_own.shape
    length = docs.shape[0]
    part = width // groups
    hidden = fc1_weight.shape[1] // groups

    x = lax.all_gather(x_own, "grp", axis=0, tiled=True)
    dy = lax.all_gather(dy_own, "grp", axis=0, tiled=True)
    vectors = (ln1_gain, ln1_bias, ln2_gain, ln2_bias, qkv_bias, dense_bias, fc2_bias)
    packed = lax.all_gather(jnp.concatenate(vectors), "grp", axis=0, tiled=False)
    cuts = np.cumsum([v.shape[0] for v in vectors])[:-1].tolist()
    gain1, bias1, gain2, bias2, bqkv, bd, b2 = (
        t.reshape(-1).astype(f32) for t in jnp.split(packed, cuts, axis=1)
    )
    bqkv = lax.dynamic_slice_in_dim(bqkv.reshape(3, groups, part), own, 1, 1).reshape(-1)
    wqkv = lax.all_to_all(
        qkv_weight.reshape(part, 3, groups, part), "grp", split_axis=2, concat_axis=0, tiled=True
    ).reshape(width, 3 * part)
    w1 = lax.all_to_all(fc1_weight, "grp", split_axis=1, concat_axis=0, tiled=True)
    wd = dense_weight
    w2 = fc2_weight

    def reduce_rows(grad):
        piece = lax.psum_scatter(grad.astype(bf16), "rep", scatter_dimension=0, tiled=True)
        return lax.all_gather(piece, "rep", axis=0, tiled=True).astype(f32)

    def reduce_columns(grad, blocks):
        cols = grad.shape[1]
        g = grad.astype(bf16).reshape(groups, reps, part // reps, cols)
        g = g.transpose(1, 0, 2, 3).reshape(width, cols)
        piece = lax.psum_scatter(g, "rep", scatter_dimension=0, tiled=True)
        piece = piece.reshape(groups, part // reps, cols)
        piece = lax.all_to_all(piece, "grp", split_axis=0, concat_axis=0, tiled=True)
        piece = piece.reshape(groups, part // reps, blocks, cols // blocks)
        piece = piece.transpose(1, 2, 0, 3).reshape(part // reps, groups * cols)
        return lax.all_gather(piece, "rep", axis=0, tiled=True).astype(f32)

    def normalize(t):
        t = t.astype(f32)
        centered = t - jnp.mean(t, axis=-1, keepdims=True)
        var = jnp.mean(centered * centered, axis=-1, keepdims=True)
        rstd = lax.rsqrt(var + EPS)
        return centered * rstd, rstd

    xhat, _ = normalize(x)
    a1 = (xhat * gain1 + bias1).astype(bf16)
    a2 = (xhat * gain2 + bias2).astype(bf16)

    dmix = dot_nt(dy, wd).astype(bf16)
    qkv = jnp.dot(a1, wqkv, preferred_element_type=f32) + bqkv
    mixed, dq, dk, dv, dbqkv = attention(qkv, dmix, docs)

    pre = jnp.dot(a2, w1, preferred_element_type=f32) + fc1_bias.astype(f32)
    act, slope = gelu_parts(pre)
    gact = act.astype(bf16)
    g_w2 = reduce_rows(dot_tn(gact, dy))
    dpre = dot_nt(dy, w2) * slope
    dbf1 = jnp.sum(dpre, axis=0)
    dpre_b = dpre.astype(bf16)
    g_w1 = reduce_columns(dot_tn(a2, dpre_b), 1)
    da2 = dot_nt(dpre_b, w1)

    g_wd = reduce_rows(dot_tn(mixed, dy))
    dqkv = jnp.concatenate([dq, dk, dv], axis=1)
    g_wqkv = reduce_columns(dot_tn(a1, dqkv), 3)
    da1 = dot_nt(dqkv, wqkv)

    branch = jnp.dot(mixed, wd, preferred_element_type=f32) + jnp.dot(
        gact, w2, preferred_element_type=f32
    )
    branch = lax.psum_scatter(branch.astype(bf16), "grp", scatter_dimension=0, tiled=True)
    out = (x_own.astype(f32) + branch.astype(f32) + (bd + b2)).astype(bf16)

    grad = (da1 * gain1 + da2 * gain2).astype(bf16)
    grad = lax.psum_scatter(grad, "grp", scatter_dimension=0, tiled=True).astype(f32)
    xhat_own, rstd_own = normalize(x_own)
    inner = (
        grad
        - jnp.mean(grad, axis=-1, keepdims=True)
        - xhat_own * jnp.mean(grad * xhat_own, axis=-1, keepdims=True)
    )
    dx = (dy_own.astype(f32) + rstd_own * inner).astype(bf16)

    wide = lambda v, n: lax.dynamic_update_slice_in_dim(jnp.zeros((n * v.shape[0],), f32), v, own * v.shape[0], 0)
    bq = lax.dynamic_update_slice(
        jnp.zeros((3, groups, part), f32), dbqkv[:3].reshape(3, 1, part), (0, own, 0)
    ).reshape(-1)
    pieces = (
        jnp.sum(da1 * xhat, axis=0),
        jnp.sum(da1, axis=0),
        jnp.sum(da2 * xhat, axis=0),
        jnp.sum(da2, axis=0),
        jnp.sum(dy_own.astype(f32), axis=0),
        bq,
        wide(dbf1, groups),
    )
    flat = jnp.concatenate([p.reshape(groups, -1) for p in pieces], axis=1)
    flat = lax.psum(flat, ("grp", "rep"))
    flat = lax.dynamic_slice_in_dim(flat, own, 1, 0)[0]
    cuts = np.cumsum([p.shape[0] // groups for p in pieces])[:-1].tolist()
    s_g1, s_b1, s_g2, s_b2, s_bd, s_bqkv, s_bf1 = jnp.split(flat, cuts)
    return (
        out[None],
        dx[None],
        s_g1,
        s_b1,
        s_g2,
        s_b2,
        g_wqkv,
        s_bqkv,
        g_wd,
        s_bd,
        g_w1,
        s_bf1,
        g_w2,
        s_bd,
    )


def solution(mesh):
    vec = P("grp")
    mat = P("grp", None)
    tok = P("rep", "grp", None)
    return jax.shard_map(
        functools.partial(body, mesh.shape["grp"], mesh.shape["rep"]),
        mesh=mesh,
        in_specs=(tok, P("rep", None), vec, vec, vec, vec, mat, vec, mat, vec, mat, vec, mat, vec, tok),
        out_specs=(tok, tok, vec, vec, vec, vec, mat, vec, mat, vec, mat, vec, mat, vec),
        check_vma=False,
    )
```

```python
import functools
import math

import jax
import jax.numpy as jnp
import numpy as np
from jax import lax
from jax.experimental import pallas as pl
from jax.experimental.pallas import tpu as pltpu
from jax.sharding import PartitionSpec as P

HEAD_DIM = 64
ROT = 16
EPS = 1e-05
NEG = -1e30
DOC_MAX = 512
PAIR = 128

f32 = jnp.float32
bf16 = jnp.bfloat16


def rotary_tables(length):
    half = ROT // 2
    freq = 10000.0 ** (-np.arange(half, dtype=np.float64) / half)
    angle = np.arange(length, dtype=np.float64)[:, None] * freq[None, :]
    cos = np.ones((length, HEAD_DIM))
    low = np.zeros((length, HEAD_DIM))
    high = np.zeros((length, HEAD_DIM))
    cos[:, :half] = np.cos(angle)
    cos[:, half : 2 * half] = np.cos(angle)
    low[:, :half] = -np.sin(angle)
    high[:, half : 2 * half] = np.sin(angle)
    reps = PAIR // HEAD_DIM
    return tuple(np.tile(t, (1, reps)).astype(np.float32) for t in (cos, low, high))


def rotate(x, cos, low, high, sign):
    half = ROT // 2
    up = pltpu.roll(x, PAIR - half, 1)
    down = pltpu.roll(x, half, 1)
    return x * cos + sign * (up * low + down * high)


def dot_nt(a, b):
    return lax.dot_general(a, b, (((1,), (1,)), ((), ())), preferred_element_type=f32)


def dot_tn(a, b):
    return lax.dot_general(a, b, (((0,), (0,)), ((), ())), preferred_element_type=f32)


def attention_kernel(
    block,
    q_ref,
    k_ref,
    v_ref,
    dmix_ref,
    drow_ref,
    dcol_ref,
    cos_ref,
    low_ref,
    high_ref,
    mix_ref,
    dq_ref,
    dk_ref,
    dv_ref,
    bias_ref,
    qs,
    ks,
    vs,
    dks,
    dvs,
):
    length = q_ref.shape[0]
    scale = HEAD_DIM ** (-0.5)
    tables = (cos_ref[...], low_ref[...], high_ref[...])
    qs[...] = rotate(q_ref[...], *tables, 1.0).astype(bf16)
    ks[...] = rotate(k_ref[...], *tables, 1.0).astype(bf16)
    vs[...] = v_ref[...].astype(bf16)
    dks[...] = jnp.zeros_like(dks)
    dvs[...] = jnp.zeros_like(dvs)
    dq_sum = jnp.zeros((1, PAIR), f32)
    reach = -(-(DOC_MAX - 1) // block)
    for i in range(length // block):
        first = max(0, i - reach) * block
        end = (i + 1) * block
        wide = end - first
        rows = pl.ds(i * block, block)
        keys = pl.ds(first, wide)
        q = qs[rows, :]
        dmix = dmix_ref[rows, :]
        k = ks[keys, :]
        v = vs[keys, :]
        qpos = i * block + lax.broadcasted_iota(jnp.int32, (block, wide), 0)
        kpos = first + lax.broadcasted_iota(jnp.int32, (block, wide), 1)
        allowed = (kpos <= qpos) & (dcol_ref[rows, :] == drow_ref[:, first:end])
        lane = lax.broadcasted_iota(jnp.int32, (block, PAIR), 1)
        wide_lane = lax.broadcasted_iota(jnp.int32, (wide, PAIR), 1)
        mix = dq = None
        for h in range(PAIR // HEAD_DIM):
            mine = (lane // HEAD_DIM) == h
            zero = jnp.zeros((block, PAIR), bf16)
            qh = jnp.where(mine, q, zero)
            dmixh = jnp.where(mine, dmix, zero)
            s = jnp.where(allowed, dot_nt(qh, k) * scale, NEG)
            top = jnp.max(s, axis=1, keepdims=True)
            e = jnp.exp(s - top)
            p = e * (1.0 / jnp.sum(e, axis=1, keepdims=True))
            pb = p.astype(bf16)
            o = jnp.dot(pb, v, preferred_element_type=f32).astype(bf16)
            o = jnp.where(mine, o, zero)
            delta = jnp.sum(o.astype(f32) * dmixh.astype(f32), axis=1, keepdims=True)
            dp = dot_nt(dmixh, v)
            ds = (p * (dp - delta) * scale).astype(bf16)
            dqh = jnp.dot(ds, k, preferred_element_type=f32)
            mix = o if h == 0 else mix + o
            dq = jnp.where(mine, dqh, 0.0) if h == 0 else jnp.where(mine, dqh, dq)
            dks[keys, :] += dot_tn(ds, qh)
            dvs[keys, :] += dot_tn(pb, dmixh)
        mix_ref[rows, :] = mix
        dq = rotate(dq, cos_ref[rows, :], low_ref[rows, :], high_ref[rows, :], -1.0)
        dq_sum = dq_sum + jnp.sum(dq, axis=0, keepdims=True)
        dq_ref[rows, :] = dq.astype(bf16)
    dk = rotate(dks[...], *tables, -1.0)
    dv = dvs[...]
    dk_ref[...] = dk.astype(bf16)
    dv_ref[...] = dv.astype(bf16)
    bias_ref[0:1, :] = dq_sum
    bias_ref[1:2, :] = jnp.sum(dk, axis=0, keepdims=True)
    bias_ref[2:3, :] = jnp.sum(dv, axis=0, keepdims=True)
    bias_ref[3:8, :] = jnp.zeros((5, PAIR), f32)


def attention(qkv, dmix, docs):
    length, width = dmix.shape
    pairs = width // PAIR
    block = 256
    col = lambda off: pl.BlockSpec((length, PAIR), lambda h: (0, off + h))
    whole = lambda shape: pl.BlockSpec(shape, lambda h: (0, 0))
    tables = [jnp.asarray(t) for t in rotary_tables(length)]
    out = lambda: jax.ShapeDtypeStruct((length, width), bf16)
    return pl.pallas_call(
        functools.partial(attention_kernel, block),
        grid=(pairs,),
        in_specs=[col(0), col(pairs), col(2 * pairs), col(0)]
        + [whole((1, length)), whole((length, 1))]
        + [whole((length, PAIR))] * 3,
        out_specs=[col(0)] * 4 + [pl.BlockSpec((8, PAIR), lambda h: (0, h))],
        out_shape=[out(), out(), out(), out(), jax.ShapeDtypeStruct((8, width), f32)],
        scratch_shapes=[pltpu.VMEM((length, PAIR), bf16)] * 3
        + [pltpu.VMEM((length, PAIR), f32)] * 2,
        compiler_params=pltpu.CompilerParams(vmem_limit_bytes=40 * 1024 * 1024),
        cost_estimate=pl.CostEstimate(
            flops=10 * length * length * width, bytes_accessed=length * width * 24, transcendentals=length * length * 4
        ),
    )(qkv, qkv, qkv, dmix, docs[None, :], docs[:, None], *tables)


def bit_of(axis, bit):
    return (lax.axis_index(axis) >> bit) & 1


def swap(t, axis, bit, size):
    return lax.ppermute(t, axis, [(i, i ^ (1 << bit)) for i in range(size)])


def scatter_sum(t, axis, size, bits, dim=0):
    shape = t.shape
    held = sorted(bits, reverse=True)
    t = t.reshape(shape[:dim] + (2,) * len(held) + shape[dim + 1 :])
    for bit in bits:
        at = dim + held.index(bit)
        mine = bit_of(axis, bit)
        send = lax.dynamic_index_in_dim(t, 1 - mine, at, keepdims=False)
        keep = lax.dynamic_index_in_dim(t, mine, at, keepdims=False)
        t = (keep.astype(f32) + swap(send, axis, bit, size).astype(f32)).astype(t.dtype)
        held.remove(bit)
    return t


def gather(t, axis, size, bits):
    shape = t.shape
    held = []
    for bit in bits:
        other = swap(t, axis, bit, size)
        low = bit_of(axis, bit) == 0
        held = sorted(held + [bit], reverse=True)
        t = jnp.stack([jnp.where(low, t, other), jnp.where(low, other, t)], axis=held.index(bit))
    return t.reshape((size,) + shape)


def gelu_parts(pre):
    cdf = 0.5 * (1.0 + lax.erf(pre * (1.0 / math.sqrt(2.0))))
    dens = jnp.exp(-0.5 * pre * pre) * (1.0 / math.sqrt(2.0 * math.pi))
    return (pre * cdf, cdf + pre * dens)


def body(
    groups,
    reps,
    hidden_in,
    doc_ids,
    ln1_gain,
    ln1_bias,
    ln2_gain,
    ln2_bias,
    qkv_weight,
    qkv_bias,
    dense_weight,
    dense_bias,
    fc1_weight,
    fc1_bias,
    fc2_weight,
    fc2_bias,
    out_grad,
):
    own = lax.axis_index("grp")
    x_own = hidden_in[0]
    dy_own = out_grad[0]
    docs = doc_ids[0]
    rows, width = x_own.shape
    length = docs.shape[0]
    part = width // groups
    hidden = fc1_weight.shape[1] // groups

    near = list(range(groups.bit_length() - 1))
    far = near[::-1]
    ring = list(range(reps.bit_length() - 1))
    turned = ring[1::-1] + ring[2:]

    x = gather(x_own, "grp", groups, far).reshape(length, width)
    dy = gather(dy_own, "grp", groups, far).reshape(length, width)
    vectors = (ln1_gain, ln1_bias, ln2_gain, ln2_bias, qkv_bias, dense_bias, fc2_bias)
    packed = gather(jnp.concatenate(vectors), "grp", groups, far)
    cuts = np.cumsum([v.shape[0] for v in vectors])[:-1].tolist()
    gain1, bias1, gain2, bias2, bqkv, bd, b2 = (
        t.reshape(-1).astype(f32) for t in jnp.split(packed, cuts, axis=1)
    )
    bqkv = lax.dynamic_slice_in_dim(bqkv.reshape(3, groups, part), own, 1, 1).reshape(-1)
    wqkv = lax.all_to_all(
        qkv_weight.reshape(part, 3, groups, part), "grp", split_axis=2, concat_axis=0, tiled=True
    ).reshape(width, 3 * part)
    w1 = lax.all_to_all(fc1_weight, "grp", split_axis=1, concat_axis=0, tiled=True)
    wd = dense_weight
    w2 = fc2_weight

    def reduce_rows(grad, order):
        g = grad.astype(bf16).reshape(reps, grad.shape[0] // reps, grad.shape[1])
        piece = scatter_sum(g, "rep", reps, order)
        return gather(piece, "rep", reps, order[::-1]).reshape(grad.shape).astype(f32)

    def reduce_columns(grad, blocks, order):
        cols = grad.shape[1]
        rows = part // reps
        g = grad.astype(bf16).reshape(groups, reps, rows, cols)
        g = scatter_sum(g, "rep", reps, order, dim=1)
        piece = jnp.zeros((rows, blocks, groups, cols // blocks), bf16)
        for k in range(groups):
            block = lax.dynamic_index_in_dim(g, own ^ k, 0, keepdims=False)
            if k:
                block = lax.ppermute(block, "grp", [(i, i ^ k) for i in range(groups)])
            block = block.reshape(rows, blocks, 1, cols // blocks)
            piece = lax.dynamic_update_slice_in_dim(piece, block, own ^ k, 2)
        piece = piece.reshape(rows, groups * cols)
        return gather(piece, "rep", reps, order[::-1]).reshape(part, -1).astype(f32)

    def normalize(t):
        t = t.astype(f32)
        centered = t - jnp.mean(t, axis=-1, keepdims=True)
        var = jnp.mean(centered * centered, axis=-1, keepdims=True)
        rstd = lax.rsqrt(var + EPS)
        return centered * rstd, rstd

    xhat, _ = normalize(x)
    a1 = (xhat * gain1 + bias1).astype(bf16)
    a2 = (xhat * gain2 + bias2).astype(bf16)

    dmix = dot_nt(dy, wd).astype(bf16)
    qkv = jnp.dot(a1, wqkv, preferred_element_type=f32) + bqkv
    mixed, dq, dk, dv, dbqkv = attention(qkv, dmix, docs)

    pre = jnp.dot(a2, w1, preferred_element_type=f32) + fc1_bias.astype(f32)
    act, slope = gelu_parts(pre)
    gact = act.astype(bf16)
    g_w2 = reduce_rows(dot_tn(gact, dy), ring)
    dpre = dot_nt(dy, w2) * slope
    dbf1 = jnp.sum(dpre, axis=0)
    dpre_b = dpre.astype(bf16)
    g_w1 = reduce_columns(dot_tn(a2, dpre_b), 1, turned)
    da2 = dot_nt(dpre_b, w1)

    g_wd = reduce_rows(dot_tn(mixed, dy), turned)
    dqkv = jnp.concatenate([dq, dk, dv], axis=1)
    g_wqkv = reduce_columns(dot_tn(a1, dqkv), 3, ring)
    da1 = dot_nt(dqkv, wqkv)

    branch = jnp.dot(mixed, wd, preferred_element_type=f32) + jnp.dot(
        gact, w2, preferred_element_type=f32
    )
    branch = scatter_sum(branch.astype(bf16).reshape(groups, rows, width), "grp", groups, near)
    out = (x_own.astype(f32) + branch.astype(f32) + (bd + b2)).astype(bf16)

    grad = (da1 * gain1 + da2 * gain2).astype(bf16)
    grad = scatter_sum(grad.reshape(groups, rows, width), "grp", groups, near).astype(f32)
    xhat_own, rstd_own = normalize(x_own)
    inner = (
        grad
        - jnp.mean(grad, axis=-1, keepdims=True)
        - xhat_own * jnp.mean(grad * xhat_own, axis=-1, keepdims=True)
    )
    dx = (dy_own.astype(f32) + rstd_own * inner).astype(bf16)

    wide = lambda v, n: lax.dynamic_update_slice_in_dim(jnp.zeros((n * v.shape[0],), f32), v, own * v.shape[0], 0)
    bq = lax.dynamic_update_slice(
        jnp.zeros((3, groups, part), f32), dbqkv[:3].reshape(3, 1, part), (0, own, 0)
    ).reshape(-1)
    pieces = (
        jnp.sum(da1 * xhat, axis=0),
        jnp.sum(da1, axis=0),
        jnp.sum(da2 * xhat, axis=0),
        jnp.sum(da2, axis=0),
        jnp.sum(dy_own.astype(f32), axis=0),
        bq,
        wide(dbf1, groups),
    )
    flat = jnp.concatenate([p.reshape(groups, -1) for p in pieces], axis=1)
    flat = scatter_sum(flat, "grp", groups, near)
    for bit in ring:
        flat = flat + swap(flat, "rep", bit, reps)
    cuts = np.cumsum([p.shape[0] // groups for p in pieces])[:-1].tolist()
    s_g1, s_b1, s_g2, s_b2, s_bd, s_bqkv, s_bf1 = jnp.split(flat, cuts)
    return (
        out[None],
        dx[None],
        s_g1,
        s_b1,
        s_g2,
        s_b2,
        g_wqkv,
        s_bqkv,
        g_wd,
        s_bd,
        g_w1,
        s_bf1,
        g_w2,
        s_bd,
    )


def solution(mesh):
    vec = P("grp")
    mat = P("grp", None)
    tok = P("rep", "grp", None)
    return jax.shard_map(
        functools.partial(body, mesh.shape["grp"], mesh.shape["rep"]),
        mesh=mesh,
        in_specs=(tok, P("rep", None), vec, vec, vec, vec, mat, vec, mat, vec, mat, vec, mat, vec, tok),
        out_specs=(tok, tok, vec, vec, vec, vec, mat, vec, mat, vec, mat, vec, mat, vec),
        check_vma=False,
    )
```

```python
import functools
import math

import jax
import jax.numpy as jnp
import numpy as np
from jax import lax
from jax.experimental import pallas as pl
from jax.experimental.pallas import tpu as pltpu
from jax.sharding import PartitionSpec as P

HEAD_DIM = 64
ROT = 16
EPS = 1e-05
NEG = -1e30
DOC_MAX = 512
PAIR = 128

f32 = jnp.float32
bf16 = jnp.bfloat16


def rotary_tables(length):
    half = ROT // 2
    freq = 10000.0 ** (-np.arange(half, dtype=np.float64) / half)
    angle = np.arange(length, dtype=np.float64)[:, None] * freq[None, :]
    cos = np.ones((length, HEAD_DIM))
    low = np.zeros((length, HEAD_DIM))
    high = np.zeros((length, HEAD_DIM))
    cos[:, :half] = np.cos(angle)
    cos[:, half : 2 * half] = np.cos(angle)
    low[:, :half] = -np.sin(angle)
    high[:, half : 2 * half] = np.sin(angle)
    reps = PAIR // HEAD_DIM
    return tuple(np.tile(t, (1, reps)).astype(np.float32) for t in (cos, low, high))


def rotate(x, cos, low, high, sign):
    half = ROT // 2
    up = pltpu.roll(x, PAIR - half, 1)
    down = pltpu.roll(x, half, 1)
    return x * cos + sign * (up * low + down * high)


def dot_nt(a, b):
    return lax.dot_general(a, b, (((1,), (1,)), ((), ())), preferred_element_type=f32)


def dot_tn(a, b):
    return lax.dot_general(a, b, (((0,), (0,)), ((), ())), preferred_element_type=f32)


def attention_kernel(
    block,
    q_ref,
    k_ref,
    v_ref,
    dmix_ref,
    drow_ref,
    dcol_ref,
    cos_ref,
    low_ref,
    high_ref,
    mix_ref,
    dq_ref,
    dk_ref,
    dv_ref,
    bias_ref,
    qs,
    ks,
    vs,
    dks,
    dvs,
):
    length = q_ref.shape[0]
    scale = HEAD_DIM ** (-0.5)
    tables = (cos_ref[...], low_ref[...], high_ref[...])
    qs[...] = rotate(q_ref[...], *tables, 1.0).astype(bf16)
    ks[...] = rotate(k_ref[...], *tables, 1.0).astype(bf16)
    vs[...] = v_ref[...].astype(bf16)
    dks[...] = jnp.zeros_like(dks)
    dvs[...] = jnp.zeros_like(dvs)
    dq_sum = jnp.zeros((1, PAIR), f32)
    reach = -(-(DOC_MAX - 1) // block)
    for i in range(length // block):
        first = max(0, i - reach) * block
        end = (i + 1) * block
        wide = end - first
        rows = pl.ds(i * block, block)
        keys = pl.ds(first, wide)
        q = qs[rows, :]
        dmix = dmix_ref[rows, :]
        k = ks[keys, :]
        v = vs[keys, :]
        qpos = i * block + lax.broadcasted_iota(jnp.int32, (block, wide), 0)
        kpos = first + lax.broadcasted_iota(jnp.int32, (block, wide), 1)
        allowed = (kpos <= qpos) & (dcol_ref[rows, :] == drow_ref[:, first:end])
        lane = lax.broadcasted_iota(jnp.int32, (block, PAIR), 1)
        wide_lane = lax.broadcasted_iota(jnp.int32, (wide, PAIR), 1)
        mix = dq = None
        for h in range(PAIR // HEAD_DIM):
            mine = (lane // HEAD_DIM) == h
            zero = jnp.zeros((block, PAIR), bf16)
            qh = jnp.where(mine, q, zero)
            dmixh = jnp.where(mine, dmix, zero)
            s = jnp.where(allowed, dot_nt(qh, k) * scale, NEG)
            top = jnp.max(s, axis=1, keepdims=True)
            e = jnp.exp(s - top)
            p = e * (1.0 / jnp.sum(e, axis=1, keepdims=True))
            pb = p.astype(bf16)
            o = jnp.dot(pb, v, preferred_element_type=f32).astype(bf16)
            o = jnp.where(mine, o, zero)
            delta = jnp.sum(o.astype(f32) * dmixh.astype(f32), axis=1, keepdims=True)
            dp = dot_nt(dmixh, v)
            ds = (p * (dp - delta) * scale).astype(bf16)
            dqh = jnp.dot(ds, k, preferred_element_type=f32)
            mix = o if h == 0 else mix + o
            dq = jnp.where(mine, dqh, 0.0) if h == 0 else jnp.where(mine, dqh, dq)
            dks[keys, :] += dot_tn(ds, qh)
            dvs[keys, :] += dot_tn(pb, dmixh)
        mix_ref[rows, :] = mix
        dq = rotate(dq, cos_ref[rows, :], low_ref[rows, :], high_ref[rows, :], -1.0)
        dq_sum = dq_sum + jnp.sum(dq, axis=0, keepdims=True)
        dq_ref[rows, :] = dq.astype(bf16)
    dk = rotate(dks[...], *tables, -1.0)
    dv = dvs[...]
    dk_ref[...] = dk.astype(bf16)
    dv_ref[...] = dv.astype(bf16)
    bias_ref[0:1, :] = dq_sum
    bias_ref[1:2, :] = jnp.sum(dk, axis=0, keepdims=True)
    bias_ref[2:3, :] = jnp.sum(dv, axis=0, keepdims=True)
    bias_ref[3:8, :] = jnp.zeros((5, PAIR), f32)


def attention(qkv, dmix, docs):
    length, width = dmix.shape
    pairs = width // PAIR
    block = 256
    col = lambda off: pl.BlockSpec((length, PAIR), lambda h: (0, off + h))
    whole = lambda shape: pl.BlockSpec(shape, lambda h: (0, 0))
    tables = [jnp.asarray(t) for t in rotary_tables(length)]
    out = lambda: jax.ShapeDtypeStruct((length, width), bf16)
    return pl.pallas_call(
        functools.partial(attention_kernel, block),
        grid=(pairs,),
        in_specs=[col(0), col(pairs), col(2 * pairs), col(0)]
        + [whole((1, length)), whole((length, 1))]
        + [whole((length, PAIR))] * 3,
        out_specs=[col(0)] * 4 + [pl.BlockSpec((8, PAIR), lambda h: (0, h))],
        out_shape=[out(), out(), out(), out(), jax.ShapeDtypeStruct((8, width), f32)],
        scratch_shapes=[pltpu.VMEM((length, PAIR), bf16)] * 3
        + [pltpu.VMEM((length, PAIR), f32)] * 2,
        compiler_params=pltpu.CompilerParams(vmem_limit_bytes=40 * 1024 * 1024),
        cost_estimate=pl.CostEstimate(
            flops=10 * length * length * width, bytes_accessed=length * width * 24, transcendentals=length * length * 4
        ),
    )(qkv, qkv, qkv, dmix, docs[None, :], docs[:, None], *tables)


def bit_of(axis, bit):
    return (lax.axis_index(axis) >> bit) & 1


def swap(t, axis, bit, size):
    return lax.ppermute(t, axis, [(i, i ^ (1 << bit)) for i in range(size)])


class Scatter:
    def __init__(self, t, axis, size, bits, dim=0):
        shape = t.shape
        self.axis, self.size, self.dim, self.left = axis, size, dim, list(bits)
        self.held = sorted(bits, reverse=True)
        self.t = t.reshape(shape[:dim] + (2,) * len(self.held) + shape[dim + 1 :])

    def begin(self):
        bit = self.left.pop(0)
        at = self.dim + self.held.index(bit)
        mine = bit_of(self.axis, bit)
        send = lax.dynamic_index_in_dim(self.t, 1 - mine, at, keepdims=False)
        self.keep = lax.dynamic_index_in_dim(self.t, mine, at, keepdims=False)
        self.other = swap(send, self.axis, bit, self.size)
        self.held.remove(bit)

    def end(self):
        self.t = (self.keep.astype(f32) + self.other.astype(f32)).astype(self.t.dtype)

    def finish(self):
        while self.left:
            self.begin()
            self.end()
        return self.t


def scatter_sum(t, axis, size, bits, dim=0):
    return Scatter(t, axis, size, bits, dim).finish()


def meet(chains, *values):
    tied = lax.optimization_barrier(tuple(c.other for c in chains) + values)
    for c, other in zip(chains, tied):
        c.other = other
        c.end()
    return tied[len(chains) :]


def gather(t, axis, size, bits):
    shape = t.shape
    held = []
    for bit in bits:
        other = swap(t, axis, bit, size)
        low = bit_of(axis, bit) == 0
        held = sorted(held + [bit], reverse=True)
        t = jnp.stack([jnp.where(low, t, other), jnp.where(low, other, t)], axis=held.index(bit))
    return t.reshape((size,) + shape)


def gelu_parts(pre):
    cdf = 0.5 * (1.0 + lax.erf(pre * (1.0 / math.sqrt(2.0))))
    dens = jnp.exp(-0.5 * pre * pre) * (1.0 / math.sqrt(2.0 * math.pi))
    return (pre * cdf, cdf + pre * dens)


def body(
    groups,
    reps,
    hidden_in,
    doc_ids,
    ln1_gain,
    ln1_bias,
    ln2_gain,
    ln2_bias,
    qkv_weight,
    qkv_bias,
    dense_weight,
    dense_bias,
    fc1_weight,
    fc1_bias,
    fc2_weight,
    fc2_bias,
    out_grad,
):
    own = lax.axis_index("grp")
    x_own = hidden_in[0]
    dy_own = out_grad[0]
    docs = doc_ids[0]
    rows, width = x_own.shape
    length = docs.shape[0]
    part = width // groups
    hidden = fc1_weight.shape[1] // groups

    near = list(range(groups.bit_length() - 1))
    far = near[::-1]
    ring = list(range(reps.bit_length() - 1))
    turned = ring[1::-1] + ring[2:]

    x = gather(x_own, "grp", groups, far).reshape(length, width)
    dy = gather(dy_own, "grp", groups, far).reshape(length, width)
    vectors = (ln1_gain, ln1_bias, ln2_gain, ln2_bias, qkv_bias, dense_bias, fc2_bias)
    packed = gather(jnp.concatenate(vectors), "grp", groups, far)
    cuts = np.cumsum([v.shape[0] for v in vectors])[:-1].tolist()
    gain1, bias1, gain2, bias2, bqkv, bd, b2 = (
        t.reshape(-1).astype(f32) for t in jnp.split(packed, cuts, axis=1)
    )
    bqkv = lax.dynamic_slice_in_dim(bqkv.reshape(3, groups, part), own, 1, 1).reshape(-1)
    def columns(weight, blocks):
        step = weight.shape[1] // blocks
        take = step // groups
        full = jnp.zeros((groups, part, take * blocks), bf16)
        for k in range(groups):
            to = own ^ k
            cut = [
                lax.dynamic_slice_in_dim(weight, c * step + to * take, take, 1) for c in range(blocks)
            ]
            cut = jnp.concatenate(cut, axis=1) if blocks > 1 else cut[0]
            if k:
                cut = lax.ppermute(cut, "grp", [(i, i ^ k) for i in range(groups)])
            full = lax.dynamic_update_index_in_dim(full, cut, to, 0)
        return full.reshape(groups * part, take * blocks)

    w1 = columns(fc1_weight, 1)
    wqkv = columns(qkv_weight, 3)
    wd = dense_weight
    w2 = fc2_weight

    def row_chain(grad, order):
        g = grad.astype(bf16).reshape(reps, grad.shape[0] // reps, grad.shape[1])
        return Scatter(g, "rep", reps, order)

    def column_chain(grad, order):
        g = grad.astype(bf16).reshape(groups, reps, part // reps, grad.shape[1])
        return Scatter(g, "rep", reps, order, dim=1)

    def to_rows(g, blocks):
        rows, cols = g.shape[1:]
        take = cols // blocks
        piece = jnp.zeros((rows, groups * cols), bf16)
        for k in range(groups):
            block = lax.dynamic_index_in_dim(g, own ^ k, 0, keepdims=False)
            if k:
                block = lax.ppermute(block, "grp", [(i, i ^ k) for i in range(groups)])
            for c in range(blocks):
                at = (0, c * groups * take + (own ^ k) * take)
                piece = lax.dynamic_update_slice(piece, block[:, c * take : (c + 1) * take], at)
        return piece

    def spread(piece, order):
        full = gather(piece, "rep", reps, order[::-1])
        return full.reshape(-1, piece.shape[-1]).astype(f32)

    def normalize(t):
        t = t.astype(f32)
        centered = t - jnp.mean(t, axis=-1, keepdims=True)
        var = jnp.mean(centered * centered, axis=-1, keepdims=True)
        rstd = lax.rsqrt(var + EPS)
        return centered * rstd, rstd

    xhat, _ = normalize(x)
    a1 = (xhat * gain1 + bias1).astype(bf16)
    a2 = (xhat * gain2 + bias2).astype(bf16)

    pre = jnp.dot(a2, w1, preferred_element_type=f32) + fc1_bias.astype(f32)
    act, slope = gelu_parts(pre)
    gact = act.astype(bf16)
    dpre = dot_nt(dy, w2) * slope
    dbf1 = jnp.sum(dpre, axis=0)
    dpre_b = dpre.astype(bf16)
    p_w2 = dot_tn(gact, dy).astype(bf16)
    p_w1 = dot_tn(a2, dpre_b).astype(bf16)
    c_w2 = row_chain(p_w2, ring)
    c_w1 = column_chain(p_w1, turned)
    c_w2.begin()
    c_w1.begin()

    dmix = dot_nt(dy, wd).astype(bf16)
    qkv = jnp.dot(a1, wqkv, preferred_element_type=f32) + bqkv
    mixed, dq, dk, dv, dbqkv = attention(qkv, dmix, docs)
    mixed, dq, dk, dv = meet((c_w2, c_w1), mixed, dq, dk, dv)

    c_w2.begin()
    c_w1.begin()
    dqkv = jnp.concatenate([dq, dk, dv], axis=1)
    p_wqkv = dot_tn(a1, dqkv).astype(bf16)
    p_wd = dot_tn(mixed, dy).astype(bf16)
    p_wqkv, p_wd = meet((c_w2, c_w1), p_wqkv, p_wd)

    c_w2.begin()
    c_w1.begin()
    c_wqkv = column_chain(p_wqkv, ring)
    c_wd = row_chain(p_wd, turned)
    c_wqkv.begin()
    c_wd.begin()
    da1 = dot_nt(dqkv, wqkv)
    da2 = dot_nt(dpre_b, w1)
    branch = jnp.dot(mixed, wd, preferred_element_type=f32) + jnp.dot(
        gact, w2, preferred_element_type=f32
    )
    grad = (da1 * gain1 + da2 * gain2).astype(bf16)
    branch, grad = meet((c_w2, c_w1, c_wqkv, c_wd), branch.astype(bf16), grad)
    g_w2 = spread(c_w2.finish(), ring)
    g_w1 = spread(to_rows(c_w1.finish(), 1), turned)
    g_wqkv = spread(to_rows(c_wqkv.finish(), 3), ring)
    g_wd = spread(c_wd.finish(), turned)

    branch = scatter_sum(branch.reshape(groups, rows, width), "grp", groups, near)
    out = (x_own.astype(f32) + branch.astype(f32) + (bd + b2)).astype(bf16)

    grad = scatter_sum(grad.reshape(groups, rows, width), "grp", groups, near).astype(f32)
    xhat_own, rstd_own = normalize(x_own)
    inner = (
        grad
        - jnp.mean(grad, axis=-1, keepdims=True)
        - xhat_own * jnp.mean(grad * xhat_own, axis=-1, keepdims=True)
    )
    dx = (dy_own.astype(f32) + rstd_own * inner).astype(bf16)

    wide = lambda v, n: lax.dynamic_update_slice_in_dim(jnp.zeros((n * v.shape[0],), f32), v, own * v.shape[0], 0)
    bq = lax.dynamic_update_slice(
        jnp.zeros((3, groups, part), f32), dbqkv[:3].reshape(3, 1, part), (0, own, 0)
    ).reshape(-1)
    pieces = (
        jnp.sum(da1 * xhat, axis=0),
        jnp.sum(da1, axis=0),
        jnp.sum(da2 * xhat, axis=0),
        jnp.sum(da2, axis=0),
        jnp.sum(dy_own.astype(f32), axis=0),
        bq,
        wide(dbf1, groups),
    )
    flat = jnp.concatenate([p.reshape(groups, -1) for p in pieces], axis=1)
    flat = scatter_sum(flat, "grp", groups, near)
    for bit in ring:
        flat = flat + swap(flat, "rep", bit, reps)
    cuts = np.cumsum([p.shape[0] // groups for p in pieces])[:-1].tolist()
    s_g1, s_b1, s_g2, s_b2, s_bd, s_bqkv, s_bf1 = jnp.split(flat, cuts)
    return (
        out[None],
        dx[None],
        s_g1,
        s_b1,
        s_g2,
        s_b2,
        g_wqkv,
        s_bqkv,
        g_wd,
        s_bd,
        g_w1,
        s_bf1,
        g_w2,
        s_bd,
    )


def solution(mesh):
    vec = P("grp")
    mat = P("grp", None)
    tok = P("rep", "grp", None)
    return jax.shard_map(
        functools.partial(body, mesh.shape["grp"], mesh.shape["rep"]),
        mesh=mesh,
        in_specs=(tok, P("rep", None), vec, vec, vec, vec, mat, vec, mat, vec, mat, vec, mat, vec, tok),
        out_specs=(tok, tok, vec, vec, vec, vec, mat, vec, mat, vec, mat, vec, mat, vec),
        check_vma=False,
    )
```
